32 devices in a mesh: dp: 4 (over z), lat: 2 (over x), lon: 4 (over y, core).
Axes of the slice: x: 2, y: 2, z: 4, core: 2. Of those that a mesh axis runs over, the one named last changes fastest.
Arguments:
- initial_state: float32 [4, 128, 16, 512], P('dp', None, 'lat', 'lon'), may hold values from -6 to 6
- cotangent: float32 [4, 128, 16, 512], P('dp', None, 'lat', 'lon'), may hold values from -6 to 6
- diffusion: float32 [128], replicated, may hold values from 0.02 to 0.2
- norm_gain: float32 [128], replicated, may hold values from 0.5 to 1.5
- weight_in: bfloat16 [1024, 128], replicated, may hold values from -0.5 to 0.5
- bias_in: float32 [1024], replicated, may hold values from -3 to 3
- weight_out: bfloat16 [128, 1024], replicated, may hold values from -0.1875 to 0.1875
Outputs:
- final_state: float32 [4, 128, 16, 512], P('dp', None, 'lat', 'lon')
- state_grad: float32 [4, 128, 16, 512], P('dp', None, 'lat', 'lon')
- grad_in: float32 [1024, 128], replicated
- grad_out: float32 [128, 1024], replicated
The draws below stay inside these ranges and needn't reach their ends.
All inputs are finite; a program needn't handle non-finite values.
Results may differ from the reference program's by a relative error of at most 0.006.
Values sent between devices are 32-bit elements; how exact they have to be, the bound alone decides.
A program may use at most 64 MiB of HBM per device.

```python
import math
import jax
import jax.numpy as jnp
from jax import lax

C = 128
H = 1024
ROLL = 2
G = 4
NLAT = 16
NLON = 512


def shard_levels(own_key, extent, shards, smallest, top_value):
    factor_of = 1.0
    for position, shards_of in shards:
        steps = jax.random.uniform(jax.random.fold_in(jax.random.fold_in(own_key, 6), position), (shards_of,), jnp.float32, smallest / len(shards), top_value / len(shards))
        factor_of = factor_of * jnp.repeat(jnp.exp(steps), extent[position] // shards_of).reshape((-1,) + (1,) * (len(extent) - 1 - position))
    return factor_of


def centred(rng, dims, spread, limit, shards=(), kind=jnp.bfloat16):
    result = jax.random.normal(rng, dims, jnp.float32) * spread
    if len(shards) > 0:
        result = shard_levels(rng, dims, shards, -0.22, 0.18) * result
    return jnp.clip(result, min=-limit, max=limit).astype(kind)


def setup_inputs(seed: int = 0) -> dict:
    key_of = jax.random.split(jax.random.key(seed), 8)
    return {
        "initial_state": centred(key_of[0], (G, C, NLAT, NLON), 1.0, 6.0, ((0, 4), (2, 2), (3, 4)), jnp.float32),
        "cotangent": centred(key_of[1], (G, C, NLAT, NLON), 1.0, 6.0, ((0, 4), (2, 2), (3, 4)), jnp.float32),
        "diffusion": jnp.clip(jnp.exp(jax.random.uniform(key_of[2], (C,), jnp.float32, math.log(0.02), math.log(0.2))), 0.02, 0.2),
        "norm_gain": jnp.clip(jax.random.uniform(key_of[3], (C,), jnp.float32, 0.5, 1.5), 0.5, 1.5),
        "weight_in": centred(key_of[4], (H, C), C ** -0.5, 0.5),
        "bias_in": centred(key_of[5], (H,), 0.5, 3.0, (), jnp.float32),
        "weight_out": centred(key_of[6], (C, H), H ** -0.5, 0.1875),
    }


EPSILON = 1e-05
CONTRACT_LAST = (((1,), (1,)), ((), ()))
CONTRACT_FIRST = (((0,), (0,)), ((), ()))

def laplace(field):
    padded = jnp.pad(field, ((0, 0), (1, 1), (0, 0)))
    return padded[:, 2:, :] + padded[:, :-2, :] + jnp.roll(field, 1, 2) + jnp.roll(field, -1, 2) - 4.0 * field

def physics(mixed, norm_gain, weight_in, bias_in, weight_out):
    inverse = lax.rsqrt(lax.optimization_barrier(jnp.mean(mixed * mixed, axis=0)) + EPSILON)
    normed = (mixed * inverse * norm_gain[:, None, None]).astype(jnp.bfloat16)
    flat_normed = normed.reshape(normed.shape[0], -1)
    pre_act = jnp.dot(weight_in, flat_normed, preferred_element_type=jnp.float32) + bias_in[:, None]
    squashed = jnp.tanh(pre_act)
    hidden = squashed.astype(jnp.bfloat16)
    update = jnp.dot(weight_out, hidden, preferred_element_type=jnp.float32)
    return (mixed + update.reshape(mixed.shape), (inverse, flat_normed, squashed, hidden))

def adjoint_step(field, adjoint, diffusion, norm_gain, weight_in, bias_in, weight_out):
    mixed = field + diffusion[:, None, None] * laplace(field)
    unused, cache = physics(mixed, norm_gain, weight_in, bias_in, weight_out)
    inverse, flat_normed, squashed, hidden = cache
    channels = field.shape[0]
    adjoint_flat = adjoint.reshape(channels, -1).astype(jnp.bfloat16)
    term_out = lax.dot_general(adjoint_flat, hidden, CONTRACT_LAST, preferred_element_type=jnp.float32)
    hidden_adj = lax.dot_general(weight_out, adjoint_flat, CONTRACT_FIRST, preferred_element_type=jnp.float32)
    pre_adj = (hidden_adj * (1.0 - squashed * squashed)).astype(jnp.bfloat16)
    term_in = lax.dot_general(pre_adj, flat_normed, CONTRACT_LAST, preferred_element_type=jnp.float32)
    normed_adj = lax.dot_general(weight_in, pre_adj, CONTRACT_FIRST, preferred_element_type=jnp.float32)
    scaled_adj = normed_adj.reshape(field.shape) * norm_gain[:, None, None]
    inner = lax.optimization_barrier(jnp.sum(scaled_adj * mixed, axis=0))
    mixed_adj = adjoint + inverse * scaled_adj - mixed * inverse ** 3 * inner / channels
    field_adj = mixed_adj + diffusion[:, None, None] * laplace(mixed_adj)
    return (field_adj, term_in, term_out)

def reference(initial_state, cotangent, diffusion, norm_gain, weight_in, bias_in, weight_out):

    def one_state(pair):
        start, seed_adj = pair
        fields = [start]
        for section in range(ROLL):
            mixed = fields[-1] + diffusion[:, None, None] * laplace(fields[-1])
            nxt, unused = physics(mixed, norm_gain, weight_in, bias_in, weight_out)
            fields.append(nxt)
        adjoint = seed_adj
        sum_in = jnp.zeros(weight_in.shape, jnp.float32)
        sum_out = jnp.zeros(weight_out.shape, jnp.float32)
        for section in reversed(range(ROLL)):
            adjoint, term_in, term_out = adjoint_step(fields[section], adjoint, diffusion, norm_gain, weight_in, bias_in, weight_out)
            sum_in = sum_in + term_in
            sum_out = sum_out + term_out
        return (fields[-1], adjoint, sum_in, sum_out)
    finals, adjoints, sums_in, sums_out = lax.map(one_state, (initial_state, cotangent))
    factor = jnp.float32(1.0 / math.sqrt(G * NLAT * NLON))
    return (finals, adjoints, lax.optimization_barrier(jnp.sum(sums_in, axis=0)) * factor, lax.optimization_barrier(jnp.sum(sums_out, axis=0)) * factor)
```

```python
import functools
import math

import jax
import jax.numpy as jnp
from jax import lax
from jax.experimental import pallas as pl
from jax.experimental.pallas import tpu as pltpu
from jax.sharding import PartitionSpec as P

EPSILON = 1e-05
MESH = pl.DeviceIdType.MESH
F32 = jnp.float32
BF16 = jnp.bfloat16
NT = (((1,), (1,)), ((), ()))


def make_plan(sizes, hidden):
    pair = 2 if sizes["lon"] % 2 == 0 else 1
    counts = {"core": pair, "high": sizes["lon"] // pair, "lat": sizes["lat"], "dp": sizes["dp"]}
    orders = (("core", "high", "lat", "dp"), ("core", "lat", "high", "dp"))
    plan, slot, sem = [], 0, 0
    for stream in range(2):
        for part, order in enumerate(orders):
            rows = hidden // len(orders)
            start = stream * hidden + part * rows
            phases = []
            length = rows
            for axis in order:
                n = counts[axis]
                if n == 1:
                    continue
                if length % (8 * n) == 0:
                    shard = length // n
                    phases.append(("scatter", axis, n, shard, slot, sem, sem + n - 1))
                    slot += (n - 1) * shard
                    sem += 2 * (n - 1)
                    length = shard
                else:
                    phases.append(("reduce", axis, n, length, slot, sem, None))
                    slot += n * length
                    sem += n - 1
            plan.append((start, rows, phases))
    return pair, plan, max(slot, 8), max(sem, 1)


def kernel(
    sizes, factor,
    x_hbm, cot_hbm, dif, gain, win_hbm, bias, wout_hbm,
    fin_hbm, sg_hbm, gin_hbm, gout_hbm,
    xin, cot, win, wout, winT, woutT, biasb,
    F0, F1, M0, M1, ADJ, MA, ADJB, NB0, NB1, INV, HID0, HID1, D0, HA, PA,
    acc, res, slots, packed, halo_lat, halo_lon, fin_v, sg_v,
    load_sem, store_sem, lat_send, lat_recv, lon_send, lon_recv, red_send, red_recv,
):
    C, R, L = xin.shape
    H = win.shape[0]
    n_lat, n_lon, n_dp = sizes["lat"], sizes["lon"], sizes["dp"]
    lat, lon, dp = lax.axis_index("lat"), lax.axis_index("lon"), lax.axis_index("dp")
    pair, plan, _, _ = make_plan(sizes, H)
    n_high = n_lon // pair
    core, high = lax.rem(lon, pair), lon // pair

    loads = [
        pltpu.make_async_copy(x_hbm.at[0], xin, load_sem.at[0]),
        pltpu.make_async_copy(win_hbm, win, load_sem.at[1]),
        pltpu.make_async_copy(wout_hbm, wout, load_sem.at[2]),
        pltpu.make_async_copy(cot_hbm.at[0], cot, load_sem.at[3]),
    ]
    for copy in loads:
        copy.start()

    barrier = pltpu.get_barrier_semaphore()
    total = 0
    for name, n, i in (("lon", n_lon, lon), ("lat", n_lat, lat), ("dp", n_dp, dp)):
        for k in range(1, n):
            pl.semaphore_signal(barrier, inc=1, device_id={name: lax.rem(i + k, n)}, device_id_type=MESH)
            total += 1

    lane = lax.broadcasted_iota(jnp.int32, (C, L), 1)

    def pack(e, src):
        out = jnp.zeros((C, L), F32)
        for r in range(R):
            row = src[r]
            first = pltpu.roll(row, r, 1) if r else row
            last = pltpu.roll(row, R + r + 1, 1)
            out = jnp.where(lane == r, first, jnp.where(lane == R + r, last, out))
        packed[e] = out.T[: 2 * R, :]

    def lat_copies(e, src):
        down = functools.partial(
            pltpu.make_async_remote_copy,
            src_ref=src.at[R - 1], dst_ref=halo_lat.at[e, 0],
            send_sem=lat_send.at[e, 0], recv_sem=lat_recv.at[e, 0],
            device_id={"lat": lax.rem(lat + 1, n_lat)}, device_id_type=MESH)
        up = functools.partial(
            pltpu.make_async_remote_copy,
            src_ref=src.at[0], dst_ref=halo_lat.at[e, 1],
            send_sem=lat_send.at[e, 1], recv_sem=lat_recv.at[e, 1],
            device_id={"lat": lax.rem(lat + n_lat - 1, n_lat)}, device_id_type=MESH)
        return down, up

    def lon_copies(e):
        right = pltpu.make_async_remote_copy(
            src_ref=packed.at[e, pl.ds(R, R)], dst_ref=halo_lon.at[e, pl.ds(0, R)],
            send_sem=lon_send.at[e, 0], recv_sem=lon_recv.at[e, 0],
            device_id={"lon": lax.rem(lon + 1, n_lon)}, device_id_type=MESH)
        left = pltpu.make_async_remote_copy(
            src_ref=packed.at[e, pl.ds(0, R)], dst_ref=halo_lon.at[e, pl.ds(R, R)],
            send_sem=lon_send.at[e, 1], recv_sem=lon_recv.at[e, 1],
            device_id={"lon": lax.rem(lon + n_lon - 1, n_lon)}, device_id_type=MESH)
        return right, left

    def send_lat(e, src):
        down, up = lat_copies(e, src)

        @pl.when(lat < n_lat - 1)
        def _():
            down().start()

        @pl.when(lat > 0)
        def _():
            up().start()

    def send_lon(e, src):
        pack(e, src)
        for copy in lon_copies(e):
            copy.start()

    def wait_halo(e, src):
        down, up = lat_copies(e, src)

        @pl.when(lat > 0)
        def _():
            down().wait_recv()

        @pl.when(lat == 0)
        def _():
            halo_lat[e, 0] = jnp.zeros((C, L), F32)

        @pl.when(lat < n_lat - 1)
        def _():
            up().wait_recv()

        @pl.when(lat == n_lat - 1)
        def _():
            halo_lat[e, 1] = jnp.zeros((C, L), F32)

        for copy in lon_copies(e):
            copy.wait_recv()

    def wait_sent(e, src):
        down, up = lat_copies(e, src)

        @pl.when(lat < n_lat - 1)
        def _():
            down().wait_send()

        @pl.when(lat > 0)
        def _():
            up().wait_send()

        for copy in lon_copies(e):
            copy.wait_send()

    def diffuse(e, src, put):
        side = halo_lon[e].T
        dT = jnp.broadcast_to(dif[...], (L, C)).T
        for r in range(R):
            here = src[r]
            above = src[r - 1] if r else halo_lat[e, 0]
            below = src[r + 1] if r < R - 1 else halo_lat[e, 1]
            west = jnp.where(lane == 0, pltpu.roll(side, L - r, 1) if r else side, pltpu.roll(here, 1, 1))
            east = jnp.where(lane == L - 1, pltpu.roll(side, L - 1 - R - r, 1), pltpu.roll(here, L - 1, 1))
            put(r, here + dT * (below + above + east + west - 4.0 * here))

    def normalise(t, r, m, nb, gT):
        inv = lax.rsqrt(jnp.sum(m * m, axis=0, keepdims=True) * (1.0 / C) + EPSILON)
        INV[t, r] = inv
        nb[:, r * L:(r + 1) * L] = (m * inv * gT).astype(BF16)

    W = 2 * L
    HB = 256

    def span(q, width):
        return pl.ds(pl.multiple_of(q * width, width), width)

    def line(axis, i_n):
        if axis == "core":
            return core, lambda p: {"lon": high * pair + p}
        if axis == "high":
            return high, lambda p: {"lon": p * pair + core}
        if axis == "lat":
            return lat, lambda p: {"lat": p}
        return dp, lambda p: {"dp": p}

    sent = []

    def substream(start, rows, phases):
        base, length = start, rows
        done = []
        for kind, axis, n, size, slot, sem, gsem in phases:
            i, device = line(axis, n)
            copies = []
            for k in range(1, n):
                p = lax.rem(i + k, n)
                if kind == "scatter":
                    src = acc.at[pl.ds(pl.multiple_of(base + p * size, 8), size)]
                    dst = slots.at[pl.ds(slot + (k - 1) * size, size)]
                else:
                    src = acc.at[pl.ds(pl.multiple_of(base, 8), size)]
                    dst = slots.at[pl.ds(pl.multiple_of(slot + i * size, 8), size)]
                copy = pltpu.make_async_remote_copy(
                    src_ref=src, dst_ref=dst, send_sem=red_send.at[sem + k - 1], recv_sem=red_recv.at[sem + k - 1],
                    device_id=device(p), device_id_type=MESH)
                copy.start()
                copies.append(copy)
            if kind == "scatter":
                sent.extend(copies)
                done.append((base, axis, n, size, gsem))
                base, length = base + i * size, size
            mine = pl.ds(pl.multiple_of(base, 8), length)
            if kind == "reduce":
                slots[pl.ds(pl.multiple_of(slot + i * size, 8), size)] = acc[mine]
            yield
            for copy in copies:
                copy.wait_recv()
            if kind == "scatter":
                value = acc[mine]
                for k in range(n - 1):
                    value = value + slots[pl.ds(slot + k * size, size)]
            else:
                for copy in copies:
                    copy.wait_send()
                value = slots[pl.ds(slot, size)]
                for k in range(1, n):
                    value = value + slots[pl.ds(slot + k * size, size)]
            acc[mine] = value
        mine = pl.ds(pl.multiple_of(base, 8), length)
        res[mine] = acc[mine] * factor
        for parent, axis, n, size, gsem in reversed(done):
            i, device = line(axis, n)
            here = pl.ds(pl.multiple_of(parent + i * size, 8), size)
            copies = []
            for k in range(1, n):
                copy = pltpu.make_async_remote_copy(
                    src_ref=res.at[here], dst_ref=res.at[here],
                    send_sem=red_send.at[gsem + k - 1], recv_sem=red_recv.at[gsem + k - 1],
                    device_id=device(lax.rem(i + k, n)), device_id_type=MESH)
                copy.start()
                copies.append(copy)
            sent.extend(copies)
            yield
            for copy in copies:
                copy.wait_recv()

    streams = [substream(*p) for p in plan]
    n_in = len(plan) // 2
    in_streams, out_streams = streams[:n_in], streams[n_in:]

    def advance(group):
        going = False
        for g in group:
            going = next(g, "end") is None or going
        return going

    loads[0].wait()
    for r in range(R):
        F0[r] = xin[:, r, :]
    for e in range(4):
        halo_lon[e, 2 * R:, :] = jnp.zeros((L - 2 * R, C), F32)
    if total:
        pl.semaphore_wait(barrier, total)
    send_lat(0, F0)
    send_lon(0, F0)
    gT = jnp.broadcast_to(gain[...], (L, C)).T
    for b in range(H // L):
        biasb[b * L:(b + 1) * L, :] = jnp.broadcast_to(bias[b:b + 1, :], (L, L)).T
    loads[1].wait()
    loads[2].wait()
    winT[...] = win[...].T
    woutT[...] = wout[...].T
    loads[3].wait()
    for r in range(R):
        a = cot[:, r, :]
        ADJ[r] = a
        ADJB[:, r * L:(r + 1) * L] = a.astype(BF16)
    wait_halo(0, F0)

    def put_m0(r, m):
        M0[r] = m
        normalise(0, r, m, NB0, gT)

    diffuse(0, F0, put_m0)

    def forward0(q, carry):
        cols = span(q, W)
        nq = NB0[:, cols]
        update = jnp.zeros((C, W), F32)
        for h in range(0, H, HB):
            b = biasb[h:h + HB, :]
            s = jnp.tanh(jnp.dot(win[h:h + HB, :], nq, preferred_element_type=F32) + jnp.concatenate([b, b], 1))
            D0[h:h + HB, cols] = 1.0 - s * s
            hid = s.astype(BF16)
            HID0[h:h + HB, cols] = hid
            update = update + jnp.dot(wout[:, h:h + HB], hid, preferred_element_type=F32)
        F1[2 * q] = M0[2 * q] + update[:, :L]
        F1[2 * q + 1] = M0[2 * q + 1] + update[:, L:]
        return carry

    lax.fori_loop(0, R // 2, forward0, 0)
    send_lat(1, F1)
    send_lon(1, F1)

    def early_adjoint(q, carry):
        cols = span(q, W)
        aq = ADJB[:, cols]
        for h in range(0, H, HB):
            HA[h:h + HB, cols] = jnp.dot(woutT[h:h + HB, :], aq, preferred_element_type=F32)
        return carry

    lax.fori_loop(0, R // 2, early_adjoint, 0)
    wait_halo(1, F1)

    def put_m1(r, m):
        M1[r] = m
        normalise(1, r, m, NB1, gT)

    diffuse(1, F1, put_m1)

    def mix(t, r, M, na, gt):
        m = M[r]
        inv = INV[t, r]
        scaled = gt * na
        inner = jnp.sum(scaled * m, axis=0, keepdims=True)
        MA[r] = ADJ[r] + inv * scaled - m * (inv * inv * inv * inner * (1.0 / C))

    def forward1(q, carry):
        cols = span(q, W)
        nq = NB1[:, cols]
        update = jnp.zeros((C, W), F32)
        na = jnp.zeros((C, W), F32)
        for h in range(0, H, HB):
            b = biasb[h:h + HB, :]
            s = jnp.tanh(jnp.dot(win[h:h + HB, :], nq, preferred_element_type=F32) + jnp.concatenate([b, b], 1))
            pa = (HA[h:h + HB, cols] * (1.0 - s * s)).astype(BF16)
            PA[h:h + HB, cols] = pa
            na = na + jnp.dot(winT[:, h:h + HB], pa, preferred_element_type=F32)
            hid = s.astype(BF16)
            HID1[h:h + HB, cols] = hid
            update = update + jnp.dot(wout[:, h:h + HB], hid, preferred_element_type=F32)
        gt = jnp.broadcast_to(gain[...], (L, C)).T
        for k in range(2):
            F0[2 * q + k] = M1[2 * q + k] + update[:, k * L:(k + 1) * L]
            mix(1, 2 * q + k, M1, na[:, k * L:(k + 1) * L], gt)
        return carry

    wait_sent(0, F0)
    lax.fori_loop(0, R // 2, forward1, 0)
    send_lat(2, MA)
    send_lon(2, MA)

    def terms_out(hid_ref, add):
        def body(j, carry):
            rows = span(j, HB)
            t = lax.dot_general(ADJB[...], hid_ref[rows, :], NT, preferred_element_type=F32)
            for k in range(HB // L):
                at = pl.ds(pl.multiple_of(H + j * HB + k * L, L), C)
                part = t[:, k * L:(k + 1) * L]
                acc[at, :] = acc[at, :] + part if add else part
            return carry
        lax.fori_loop(0, H // HB, body, 0)

    def terms_in(nb, add, lo, hi):
        def body(j, carry):
            rows = span(j, HB)
            t = lax.dot_general(PA[rows, :], nb[...], NT, preferred_element_type=F32)
            acc[rows, :] = acc[rows, :] + t if add else t
            return carry
        lax.fori_loop(lo, hi, body, 0)

    terms_out(HID1, False)
    terms_in(NB1, False, 0, H // HB)
    for r in range(R):
        fin_v[:, r, :] = F0[r]
    fin_store = pltpu.make_async_copy(fin_v, fin_hbm.at[0], store_sem.at[0])
    fin_store.start()
    wait_halo(2, MA)

    def put_adj(r, a):
        ADJ[r] = a
        ADJB[:, r * L:(r + 1) * L] = a.astype(BF16)

    diffuse(2, MA, put_adj)
    terms_out(HID0, True)
    advance(out_streams)

    def back0(q, carry):
        cols = span(q, W)
        aq = ADJB[:, cols]
        for h in range(0, H, HB):
            ha = jnp.dot(woutT[h:h + HB, :], aq, preferred_element_type=F32)
            PA[h:h + HB, cols] = (ha * D0[h:h + HB, cols]).astype(BF16)
        return carry

    lax.fori_loop(0, R // 2, back0, 0)
    advance(out_streams)
    blocks = H // HB
    for s, g in enumerate(in_streams):
        terms_in(NB0, True, s * blocks // n_in, (s + 1) * blocks // n_in)
        next(g, None)
    wait_sent(2, MA)

    def back1(q, carry):
        cols = span(q, W)
        na = jnp.dot(winT[...], PA[:, cols], preferred_element_type=F32)
        gt = jnp.broadcast_to(gain[...], (L, C)).T
        for k in range(2):
            mix(0, 2 * q + k, M0, na[:, k * L:(k + 1) * L], gt)
        return carry

    lax.fori_loop(0, R // 2, back1, 0)
    send_lat(3, MA)
    send_lon(3, MA)
    advance(out_streams)
    advance(in_streams)
    wait_halo(3, MA)

    def put_grad(r, a):
        sg_v[:, r, :] = a

    diffuse(3, MA, put_grad)
    sg_store = pltpu.make_async_copy(sg_v, sg_hbm.at[0], store_sem.at[1])
    sg_store.start()
    stores = [fin_store, sg_store]
    out_going = in_going = True
    while out_going or in_going:
        if out_going:
            out_going = advance(out_streams)
            if not out_going:
                for b in range(H // L):
                    copy = pltpu.make_async_copy(
                        res.at[pl.ds(H + b * L, C)], gout_hbm.at[:, pl.ds(b * L, L)], store_sem.at[3 + b])
                    copy.start()
                    stores.append(copy)
        if in_going:
            in_going = advance(in_streams)
            if not in_going:
                copy = pltpu.make_async_copy(res.at[pl.ds(0, H)], gin_hbm, store_sem.at[2])
                copy.start()
                stores.append(copy)
    for copy in sent:
        copy.wait_send()
    wait_sent(1, F1)
    wait_sent(3, MA)
    for copy in stores:
        copy.wait()


def solution(mesh):
    sizes = {name: mesh.shape[name] for name in ("dp", "lat", "lon")}
    state = P("dp", None, "lat", "lon")

    def on_device(initial_state, cotangent, diffusion, norm_gain, weight_in, bias_in, weight_out):
        _, C, R, L = initial_state.shape
        H = weight_in.shape[0]
        _, _, n_slots, n_sems = make_plan(sizes, H)
        columns = sizes["dp"] * sizes["lat"] * sizes["lon"] * R * L
        factor = 1.0 / math.sqrt(columns)
        N = R * L
        any_spec = pl.BlockSpec(memory_space=pl.ANY)
        vmem_spec = pl.BlockSpec(memory_space=pltpu.VMEM)
        tile = pltpu.VMEM((R, C, L), F32)
        scratch = [
            pltpu.VMEM((C, R, L), F32), pltpu.VMEM((C, R, L), F32),
            pltpu.VMEM((H, C), BF16), pltpu.VMEM((C, H), BF16),
            pltpu.VMEM((C, H), BF16), pltpu.VMEM((H, C), BF16),
            pltpu.VMEM((H, L), F32),
            tile, tile, tile, tile, tile, tile,
            pltpu.VMEM((C, N), BF16), pltpu.VMEM((C, N), BF16), pltpu.VMEM((C, N), BF16),
            pltpu.VMEM((2, R, 1, L), F32),
            pltpu.VMEM((H, N), BF16), pltpu.VMEM((H, N), BF16),
            pltpu.VMEM((H, N), F32), pltpu.VMEM((H, N), F32), pltpu.VMEM((H, N), BF16),
            pltpu.VMEM((2 * H, C), F32), pltpu.VMEM((2 * H, C), F32), pltpu.VMEM((n_slots, C), F32),
            pltpu.VMEM((4, 2 * R, C), F32), pltpu.VMEM((4, 2, C, L), F32), pltpu.VMEM((4, L, C), F32),
            pltpu.VMEM((C, R, L), F32), pltpu.VMEM((C, R, L), F32),
            pltpu.SemaphoreType.DMA((4,)), pltpu.SemaphoreType.DMA((3 + H // L,)),
            pltpu.SemaphoreType.DMA((4, 2)), pltpu.SemaphoreType.DMA((4, 2)),
            pltpu.SemaphoreType.DMA((4, 2)), pltpu.SemaphoreType.DMA((4, 2)),
            pltpu.SemaphoreType.DMA((n_sems,)), pltpu.SemaphoreType.DMA((n_sems,)),
        ]
        return pl.pallas_call(
            functools.partial(kernel, sizes, factor),
            out_shape=(
                jax.ShapeDtypeStruct(initial_state.shape, F32), jax.ShapeDtypeStruct(initial_state.shape, F32),
                jax.ShapeDtypeStruct((H, C), F32), jax.ShapeDtypeStruct((C, H), F32),
            ),
            in_specs=[any_spec, any_spec, vmem_spec, vmem_spec, any_spec, vmem_spec, any_spec],
            out_specs=(any_spec,) * 4,
            scratch_shapes=scratch,
            compiler_params=pltpu.CompilerParams(
                collective_id=0, has_side_effects=True, vmem_limit_bytes=50 * 1024 * 1024),
            cost_estimate=pl.CostEstimate(flops=24 * H * C * N, bytes_accessed=4 * 1024 * 1024, transcendentals=2 * H * N),
        )(
            initial_state, cotangent, diffusion.reshape(1, C), norm_gain.reshape(1, C),
            weight_in, bias_in.reshape(H // L, L), weight_out,
        )

    return jax.shard_map(
        on_device, mesh=mesh, in_specs=(state, state, P(), P(), P(), P(), P()),
        out_specs=(state, state, P(), P()), check_vma=False,
    )
```

```python
import functools
import math

import jax
import jax.numpy as jnp
from jax import lax
from jax.experimental import pallas as pl
from jax.experimental.pallas import tpu as pltpu
from jax.sharding import PartitionSpec as P

EPSILON = 1e-05
MESH = pl.DeviceIdType.MESH
F32 = jnp.float32
BF16 = jnp.bfloat16
NT = (((1,), (1,)), ((), ()))
PARTS = 2
UNROLL = True


def make_plan(sizes, hidden):
    pair = 2 if sizes["lon"] % 2 == 0 else 1
    counts = {"core": pair, "plane": sizes["lon"] // pair * sizes["lat"], "dp": sizes["dp"]}
    orders = (("core", "plane", "dp"),) * PARTS
    plan, slot, sem = [], 0, 0
    for stream in range(2):
        for part, order in enumerate(orders):
            rows = hidden // len(orders)
            start = stream * hidden + part * rows
            phases = []
            length = rows
            for axis in order:
                n = counts[axis]
                if n == 1:
                    continue
                if length % (8 * n) == 0:
                    shard = length // n
                    phases.append(("scatter", axis, n, shard, slot, sem, sem + n - 1))
                    slot += (n - 1) * shard
                    sem += 2 * (n - 1)
                    length = shard
                else:
                    phases.append(("reduce", axis, n, length, slot, sem, None))
                    slot += n * length
                    sem += n - 1
            plan.append((start, rows, phases))
    return pair, plan, max(slot, 8), max(sem, 1)


def kernel(
    sizes, factor,
    x_hbm, cot_hbm, dif, gain, win_hbm, bias, wout_hbm,
    fin_v, sg_v, gin, gout,
    xin, cot, win, wout, winT, woutT, biasb,
    F0, F1, M0, M1, ADJ, MA, ADJB, NB0, NB1, INV, HID0, HID1, D0, HA, PA,
    acc, res, slots, packed, halo_lat, halo_lon,
    load_sem, lat_send, lat_recv, lon_send, lon_recv, red_send, red_recv,
):
    C, R, L = xin.shape
    H = win.shape[0]
    n_lat, n_lon, n_dp = sizes["lat"], sizes["lon"], sizes["dp"]
    lat, lon, dp = lax.axis_index("lat"), lax.axis_index("lon"), lax.axis_index("dp")
    pair, plan, _, _ = make_plan(sizes, H)
    n_high = n_lon // pair
    core, high = lax.rem(lon, pair), lon // pair

    loads = [
        pltpu.make_async_copy(x_hbm.at[0], xin, load_sem.at[0]),
        pltpu.make_async_copy(win_hbm, win, load_sem.at[1]),
        pltpu.make_async_copy(wout_hbm, wout, load_sem.at[2]),
        pltpu.make_async_copy(cot_hbm.at[0], cot, load_sem.at[3]),
    ]
    for copy in loads:
        copy.start()

    barrier = pltpu.get_barrier_semaphore()
    greet = [{"lon": lax.rem(lon + 1, n_lon)}, {"lon": lax.rem(lon + n_lon - 1, n_lon)}]
    plane, n_plane = lat * n_high + high, n_lat * n_high
    for k in range(1, n_plane):
        p = lax.rem(plane + k, n_plane)
        greet.append({"lat": p // n_high, "lon": lax.rem(p, n_high) * pair + core})
    for k in range(1, n_dp):
        greet.append({"dp": lax.rem(dp + k, n_dp)})
    for device in greet:
        pl.semaphore_signal(barrier, inc=1, device_id=device, device_id_type=MESH)

    lane = lax.broadcasted_iota(jnp.int32, (C, L), 1)

    def pack(e, src):
        out = jnp.zeros((C, L), F32)
        for r in range(R):
            row = src[r]
            first = pltpu.roll(row, r, 1) if r else row
            last = pltpu.roll(row, R + r + 1, 1)
            out = jnp.where(lane == r, first, jnp.where(lane == R + r, last, out))
        packed[e] = out.T[: 2 * R, :]

    def lat_copies(e, src):
        down = functools.partial(
            pltpu.make_async_remote_copy,
            src_ref=src.at[R - 1], dst_ref=halo_lat.at[e, 0],
            send_sem=lat_send.at[e, 0], recv_sem=lat_recv.at[e, 0],
            device_id={"lat": lax.rem(lat + 1, n_lat)}, device_id_type=MESH)
        up = functools.partial(
            pltpu.make_async_remote_copy,
            src_ref=src.at[0], dst_ref=halo_lat.at[e, 1],
            send_sem=lat_send.at[e, 1], recv_sem=lat_recv.at[e, 1],
            device_id={"lat": lax.rem(lat + n_lat - 1, n_lat)}, device_id_type=MESH)
        return down, up

    def lon_copies(e):
        right = pltpu.make_async_remote_copy(
            src_ref=packed.at[e, pl.ds(R, R)], dst_ref=halo_lon.at[e, pl.ds(0, R)],
            send_sem=lon_send.at[e, 0], recv_sem=lon_recv.at[e, 0],
            device_id={"lon": lax.rem(lon + 1, n_lon)}, device_id_type=MESH)
        left = pltpu.make_async_remote_copy(
            src_ref=packed.at[e, pl.ds(0, R)], dst_ref=halo_lon.at[e, pl.ds(R, R)],
            send_sem=lon_send.at[e, 1], recv_sem=lon_recv.at[e, 1],
            device_id={"lon": lax.rem(lon + n_lon - 1, n_lon)}, device_id_type=MESH)
        return right, left

    def send_lat(e, src):
        down, up = lat_copies(e, src)

        @pl.when(lat < n_lat - 1)
        def _():
            down().start()

        @pl.when(lat > 0)
        def _():
            up().start()

    def send_lon(e):
        for copy in lon_copies(e):
            copy.start()

    def wait_halo(e, src):
        down, up = lat_copies(e, src)

        @pl.when(lat > 0)
        def _():
            down().wait_recv()

        @pl.when(lat == 0)
        def _():
            halo_lat[e, 0] = jnp.zeros((C, L), F32)

        @pl.when(lat < n_lat - 1)
        def _():
            up().wait_recv()

        @pl.when(lat == n_lat - 1)
        def _():
            halo_lat[e, 1] = jnp.zeros((C, L), F32)

        for copy in lon_copies(e):
            copy.wait_recv()

    def wait_sent(e, src):
        down, up = lat_copies(e, src)

        @pl.when(lat < n_lat - 1)
        def _():
            down().wait_send()

        @pl.when(lat > 0)
        def _():
            up().wait_send()

        for copy in lon_copies(e):
            copy.wait_send()

    def diffuse(e, src, put):
        side = halo_lon[e].T
        dT = jnp.broadcast_to(dif[...], (L, C)).T
        for r in range(R):
            here = src[r]
            above = src[r - 1] if r else halo_lat[e, 0]
            below = src[r + 1] if r < R - 1 else halo_lat[e, 1]
            west = jnp.where(lane == 0, pltpu.roll(side, L - r, 1) if r else side, pltpu.roll(here, 1, 1))
            east = jnp.where(lane == L - 1, pltpu.roll(side, L - 1 - R - r, 1), pltpu.roll(here, L - 1, 1))
            put(r, here + dT * (below + above + east + west - 4.0 * here))

    def normalise(t, r, m, nb, gT):
        inv = lax.rsqrt(jnp.sum(m * m, axis=0, keepdims=True) * (1.0 / C) + EPSILON)
        INV[t, r] = inv
        nb[:, r * L:(r + 1) * L] = (m * inv * gT).astype(BF16)

    W = 2 * L
    HB = 256

    def span(q, width):
        return pl.ds(pl.multiple_of(q * width, width), width)

    def loop(lo, hi, body):
        lax.fori_loop(lo, hi, body, 0, unroll=UNROLL)

    def line(axis, i_n):
        if axis == "core":
            return core, lambda p: {"lon": high * pair + p}
        if axis == "plane":
            return lat * n_high + high, lambda p: {
                "lat": p // n_high, "lon": lax.rem(p, n_high) * pair + core}
        return dp, lambda p: {"dp": p}

    sent = []

    def substream(start, rows, phases):
        base, length = start, rows
        done = []
        for kind, axis, n, size, slot, sem, gsem in phases:
            i, device = line(axis, n)
            copies = []
            for k in range(1, n):
                p = lax.rem(i + k, n)
                if kind == "scatter":
                    src = acc.at[pl.ds(pl.multiple_of(base + p * size, 8), size)]
                    dst = slots.at[pl.ds(slot + (k - 1) * size, size)]
                else:
                    src = acc.at[pl.ds(pl.multiple_of(base, 8), size)]
                    dst = slots.at[pl.ds(pl.multiple_of(slot + i * size, 8), size)]
                copy = pltpu.make_async_remote_copy(
                    src_ref=src, dst_ref=dst, send_sem=red_send.at[sem + k - 1], recv_sem=red_recv.at[sem + k - 1],
                    device_id=device(p), device_id_type=MESH)
                copy.start()
                copies.append(copy)
            if kind == "scatter":
                sent.extend(copies)
                done.append((base, axis, n, size, gsem))
                base, length = base + i * size, size
            mine = pl.ds(pl.multiple_of(base, 8), length)
            if kind == "reduce":
                slots[pl.ds(pl.multiple_of(slot + i * size, 8), size)] = acc[mine]
            yield
            for copy in copies:
                copy.wait_recv()
            if kind == "scatter":
                value = acc[mine]
                for k in range(n - 1):
                    value = value + slots[pl.ds(slot + k * size, size)]
            else:
                for copy in copies:
                    copy.wait_send()
                value = slots[pl.ds(slot, size)]
                for k in range(1, n):
                    value = value + slots[pl.ds(slot + k * size, size)]
            acc[mine] = value
        mine = pl.ds(pl.multiple_of(base, 8), length)
        res[mine] = acc[mine] * factor
        for parent, axis, n, size, gsem in reversed(done):
            i, device = line(axis, n)
            here = pl.ds(pl.multiple_of(parent + i * size, 8), size)
            copies = []
            for k in range(1, n):
                copy = pltpu.make_async_remote_copy(
                    src_ref=res.at[here], dst_ref=res.at[here],
                    send_sem=red_send.at[gsem + k - 1], recv_sem=red_recv.at[gsem + k - 1],
                    device_id=device(lax.rem(i + k, n)), device_id_type=MESH)
                copy.start()
                copies.append(copy)
            sent.extend(copies)
            yield
            for copy in copies:
                copy.wait_recv()

    streams = [substream(*p) for p in plan]
    n_in = len(plan) // 2
    in_streams, out_streams = streams[:n_in], streams[n_in:]

    def advance(group):
        going = False
        for g in group:
            going = next(g, "end") is None or going
        return going

    for e in range(4):
        halo_lon[e, 2 * R:, :] = jnp.zeros((L - 2 * R, C), F32)
    gT = jnp.broadcast_to(gain[...], (L, C)).T
    for b in range(H // L):
        biasb[b * L:(b + 1) * L, :] = jnp.broadcast_to(bias[b:b + 1, :], (L, L)).T
    loads[0].wait()
    for r in range(R):
        F0[r] = xin[:, r, :]
    pack(0, F0)
    loads[1].wait()
    loads[2].wait()
    winT[...] = win[...].T
    woutT[...] = wout[...].T
    pl.semaphore_wait(barrier, len(greet))
    send_lat(0, F0)
    send_lon(0)
    loads[3].wait()
    for r in range(R):
        a = cot[:, r, :]
        ADJ[r] = a
        ADJB[:, r * L:(r + 1) * L] = a.astype(BF16)

    def early_adjoint(q, carry):
        cols = span(q, W)
        aq = ADJB[:, cols]
        for h in range(0, H, HB):
            HA[h:h + HB, cols] = jnp.dot(woutT[h:h + HB, :], aq, preferred_element_type=F32)
        return carry

    loop(0, R // 4, early_adjoint)
    wait_halo(0, F0)

    def put_m0(r, m):
        M0[r] = m
        normalise(0, r, m, NB0, gT)

    diffuse(0, F0, put_m0)

    def forward0(q, carry):
        cols = span(q, W)
        nq = NB0[:, cols]
        update = jnp.zeros((C, W), F32)
        for h in range(0, H, HB):
            b = biasb[h:h + HB, :]
            s = jnp.tanh(jnp.dot(win[h:h + HB, :], nq, preferred_element_type=F32) + jnp.concatenate([b, b], 1))
            D0[h:h + HB, cols] = 1.0 - s * s
            hid = s.astype(BF16)
            HID0[h:h + HB, cols] = hid
            update = update + jnp.dot(wout[:, h:h + HB], hid, preferred_element_type=F32)
        F1[2 * q] = M0[2 * q] + update[:, :L]
        F1[2 * q + 1] = M0[2 * q + 1] + update[:, L:]
        return carry

    loop(0, R // 2, forward0)
    send_lat(1, F1)
    pack(1, F1)
    send_lon(1)

    loop(R // 4, R // 2, early_adjoint)
    wait_halo(1, F1)

    def put_m1(r, m):
        M1[r] = m
        normalise(1, r, m, NB1, gT)

    diffuse(1, F1, put_m1)

    def mix(t, r, M, na, gt):
        m = M[r]
        inv = INV[t, r]
        scaled = gt * na
        inner = jnp.sum(scaled * m, axis=0, keepdims=True)
        MA[r] = ADJ[r] + inv * scaled - m * (inv * inv * inv * inner * (1.0 / C))

    def forward1(q, carry):
        cols = span(q, W)
        nq = NB1[:, cols]
        update = jnp.zeros((C, W), F32)
        na = jnp.zeros((C, W), F32)
        for h in range(0, H, HB):
            b = biasb[h:h + HB, :]
            s = jnp.tanh(jnp.dot(win[h:h + HB, :], nq, preferred_element_type=F32) + jnp.concatenate([b, b], 1))
            pa = (HA[h:h + HB, cols] * (1.0 - s * s)).astype(BF16)
            PA[h:h + HB, cols] = pa
            na = na + jnp.dot(winT[:, h:h + HB], pa, preferred_element_type=F32)
            hid = s.astype(BF16)
            HID1[h:h + HB, cols] = hid
            update = update + jnp.dot(wout[:, h:h + HB], hid, preferred_element_type=F32)
        gt = jnp.broadcast_to(gain[...], (L, C)).T
        for k in range(2):
            F0[2 * q + k] = M1[2 * q + k] + update[:, k * L:(k + 1) * L]
            mix(1, 2 * q + k, M1, na[:, k * L:(k + 1) * L], gt)
        return carry

    wait_sent(0, F0)
    loop(0, R // 2, forward1)
    send_lat(2, MA)
    pack(2, MA)
    send_lon(2)

    def terms_out(hid_ref, add):
        def body(j, carry):
            rows = span(j, HB)
            t = lax.dot_general(ADJB[...], hid_ref[rows, :], NT, preferred_element_type=F32)
            for k in range(HB // L):
                at = pl.ds(pl.multiple_of(H + j * HB + k * L, L), C)
                part = t[:, k * L:(k + 1) * L]
                acc[at, :] = acc[at, :] + part if add else part
            return carry
        loop(0, H // HB, body)

    def terms_in(nb, add, lo, hi):
        def body(j, carry):
            rows = span(j, HB)
            t = lax.dot_general(PA[rows, :], nb[...], NT, preferred_element_type=F32)
            acc[rows, :] = acc[rows, :] + t if add else t
            return carry
        loop(lo, hi, body)

    terms_out(HID1, False)
    terms_in(NB1, False, 0, H // HB)
    for r in range(R):
        fin_v[0, :, r, :] = F0[r]
    wait_halo(2, MA)

    def put_adj(r, a):
        ADJ[r] = a
        ADJB[:, r * L:(r + 1) * L] = a.astype(BF16)

    diffuse(2, MA, put_adj)
    terms_out(HID0, True)
    advance(out_streams)

    def back0(q, carry):
        cols = span(q, W)
        aq = ADJB[:, cols]
        for h in range(0, H, HB):
            ha = jnp.dot(woutT[h:h + HB, :], aq, preferred_element_type=F32)
            PA[h:h + HB, cols] = (ha * D0[h:h + HB, cols]).astype(BF16)
        return carry

    loop(0, R // 2, back0)
    advance(out_streams)
    blocks = H // HB
    for s, g in enumerate(in_streams):
        terms_in(NB0, True, s * blocks // n_in, (s + 1) * blocks // n_in)
        next(g, None)
    wait_sent(2, MA)

    def back1(q, carry):
        cols = span(q, W)
        na = jnp.dot(winT[...], PA[:, cols], preferred_element_type=F32)
        gt = jnp.broadcast_to(gain[...], (L, C)).T
        for k in range(2):
            mix(0, 2 * q + k, M0, na[:, k * L:(k + 1) * L], gt)
        return carry

    loop(0, R // 2, back1)
    send_lat(3, MA)
    pack(3, MA)
    send_lon(3)
    advance(out_streams)
    advance(in_streams)
    wait_halo(3, MA)

    def put_grad(r, a):
        sg_v[0, :, r, :] = a

    diffuse(3, MA, put_grad)
    while advance(out_streams + in_streams):
        pass
    gin[...] = res[0:H]
    for b in range(H // L):
        gout[:, b * L:(b + 1) * L] = res[H + b * L:H + b * L + C]
    for copy in sent:
        copy.wait_send()
    wait_sent(1, F1)
    wait_sent(3, MA)


def solution(mesh):
    sizes = {name: mesh.shape[name] for name in ("dp", "lat", "lon")}
    state = P("dp", None, "lat", "lon")

    def on_device(initial_state, cotangent, diffusion, norm_gain, weight_in, bias_in, weight_out):
        _, C, R, L = initial_state.shape
        H = weight_in.shape[0]
        _, _, n_slots, n_sems = make_plan(sizes, H)
        columns = sizes["dp"] * sizes["lat"] * sizes["lon"] * R * L
        factor = 1.0 / math.sqrt(columns)
        N = R * L
        vmem_spec = pl.BlockSpec(memory_space=pltpu.VMEM)
        tile = pltpu.VMEM((R, C, L), F32)
        scratch = [
            pltpu.VMEM((C, R, L), F32), pltpu.VMEM((C, R, L), F32),
            pltpu.VMEM((H, C), BF16), pltpu.VMEM((C, H), BF16),
            pltpu.VMEM((C, H), BF16), pltpu.VMEM((H, C), BF16),
            pltpu.VMEM((H, L), F32),
            tile, tile, tile, tile, tile, tile,
            pltpu.VMEM((C, N), BF16), pltpu.VMEM((C, N), BF16), pltpu.VMEM((C, N), BF16),
            pltpu.VMEM((2, R, 1, L), F32),
            pltpu.VMEM((H, N), BF16), pltpu.VMEM((H, N), BF16),
            pltpu.VMEM((H, N), F32), pltpu.VMEM((H, N), F32), pltpu.VMEM((H, N), BF16),
            pltpu.VMEM((2 * H, C), F32), pltpu.VMEM((2 * H, C), F32), pltpu.VMEM((n_slots, C), F32),
            pltpu.VMEM((4, 2 * R, C), F32), pltpu.VMEM((4, 2, C, L), F32), pltpu.VMEM((4, L, C), F32),
            pltpu.SemaphoreType.DMA((4,)),
            pltpu.SemaphoreType.DMA((4, 2)), pltpu.SemaphoreType.DMA((4, 2)),
            pltpu.SemaphoreType.DMA((4, 2)), pltpu.SemaphoreType.DMA((4, 2)),
            pltpu.SemaphoreType.DMA((n_sems,)), pltpu.SemaphoreType.DMA((n_sems,)),
        ]
        shape = jax.ShapeDtypeStruct(initial_state.shape, F32)
        hbm_spec = pl.BlockSpec(memory_space=pltpu.HBM)
        return pl.pallas_call(
            functools.partial(kernel, sizes, factor),
            out_shape=(shape, shape, jax.ShapeDtypeStruct((H, C), F32), jax.ShapeDtypeStruct((C, H), F32)),
            in_specs=[hbm_spec, hbm_spec, vmem_spec, vmem_spec, hbm_spec, vmem_spec, hbm_spec],
            out_specs=(vmem_spec,) * 4,
            scratch_shapes=scratch,
            compiler_params=pltpu.CompilerParams(
                collective_id=0, has_side_effects=True, vmem_limit_bytes=60 * 1024 * 1024),
            cost_estimate=pl.CostEstimate(flops=24 * H * C * N, bytes_accessed=4 * 1024 * 1024, transcendentals=2 * H * N),
        )(
            initial_state, cotangent, diffusion.reshape(1, C), norm_gain.reshape(1, C),
            weight_in, bias_in.reshape(H // L, L), weight_out,
        )

    return jax.shard_map(
        on_device, mesh=mesh, in_specs=(state, state, P(), P(), P(), P(), P()),
        out_specs=(state, state, P(), P()), check_vma=False,
    )
```
